32 devices in a mesh: graphs: 2 (over x), dom: 16 (over z, y, core).
Axes of the slice: x: 2, y: 2, z: 4, core: 2. Of those that a mesh axis runs over, the one named last changes fastest.
Arguments:
- node_feats: float32 [4096, 256], P(('graphs', 'dom')), parts along dimension 0, may hold values from -6 to 6
- norm_gain: float32 [256], replicated, may hold values from 0.1 to 1.9
- w_query: bfloat16 [256, 256], replicated, may hold values from -32 to 32
- w_key: bfloat16 [256, 256], replicated, may hold values from -1 to 1
- w_value: bfloat16 [256, 256], replicated, may hold values from -0.375 to 0.375
- w_out: bfloat16 [256, 256], replicated, may hold values from -0.75 to 0.75
- msg_src_w: bfloat16 [256, 256], replicated, may hold values from -0.25 to 0.25
- msg_dst_w: bfloat16 [256, 256], replicated, may hold values from -0.25 to 0.25
- msg_bias: float32 [256], replicated, may hold values from -4 to 4
- msg_out_w: bfloat16 [256, 256], replicated, may hold values from -0.25 to 0.25
- msg_out_bias: float32 [256], replicated, may hold values from -3 to 3
- mlp_gain: float32 [256], replicated, may hold values from 0.1 to 1.9
- mlp_up: bfloat16 [256, 1024], replicated, may hold values from -0.375 to 0.375
- mlp_down: bfloat16 [1024, 256], replicated, may hold values from -0.1875 to 0.1875
- send_list: int32 [32, 16, 4], P(('graphs', 'dom')), parts along dimension 0, may hold values from 0 to 127
- send_count: int32 [32, 16], P('graphs', 'dom'), parts along dimension 0, may hold values from 0 to 4, as said below
- edge_src: int32 [32, 8, 128], P(('graphs', 'dom')), parts along dimension 0, may hold values from 0 to 191
- edge_dst: int32 [32, 8, 128], P(('graphs', 'dom')), parts along dimension 0, may hold values from 0 to 127
- edge_count: int32 [32], P(('graphs', 'dom')), parts along dimension 0, may hold values from 256 to 1024, as said below
Outputs:
- out_feats: float32 [4096, 256], P(('graphs', 'dom')), parts along dimension 0
The draws below stay inside these ranges and needn't reach their ends.
There are 2 independent parts, one for each index of `graphs`. The reference program is written for one: setup_inputs(seed, part) draws one part's arguments, and reference() takes and returns one part's arrays. A program takes and returns all parts, laid end to end along the dimension named above; an argument that names none is the same for every part. Nothing has to cross between parts.
Inputs may be any that keep to these rules, and one draw needn't show every extreme that they name: `send_list`: entries in slots at or past the count are arbitrary local rows. `send_count`: some sender fills all 4 slots to some receiver. `edge_src`: slots below 128 are local nodes; slot 128 + p * 4 + j is slot j of the rows received from partition p. `edge_count`: live edge slots come first in a partition's order; some partition has all 1024 slots live.
All inputs are finite; a program needn't handle non-finite values.
Results may differ from the reference program's by a relative error of at most 0.0057.
Values may be sent and summed in bfloat16 or wider, within the bound.
A program may use at most 64 MiB of HBM per device.

```python
import math
import jax
import jax.numpy as jnp
from jax import lax

D = 256
HEADS = 8
FF = 1024
NODE_DEV = 128
BMAX = 4
ETILES = 8
EDGE_TILE = 128
NODES = 2048
N_DOM = 16


def paired_weights(key):
    base_key = jax.random.fold_in(key, 7001)
    first_key, second_key, third_key = jax.random.split(base_key, 3)
    factor = D ** (-0.5)
    key_weights = jax.random.truncated_normal(first_key, -4.0, 4.0, (D, D), jnp.float32) * factor
    head_spread = jnp.exp(jax.random.uniform(third_key, (HEADS,), jnp.float32, math.log(2.4), math.log(3.2)))
    spread_columns = jnp.repeat(head_spread, D // HEADS)
    random_query = jax.random.truncated_normal(second_key, -4.0, 4.0, (D, D), jnp.float32) * factor * spread_columns[None, :]
    query_weights = random_query
    return (query_weights, key_weights)


def draw_w_query(key, part):
    return paired_weights(key)[0].astype(jnp.bfloat16)


def draw_w_key(key, part):
    return paired_weights(key)[1].astype(jnp.bfloat16)


def draw_send_count(key, part):
    base_key = jax.random.fold_in(key, 7101)
    first_key, second_key = jax.random.split(base_key)
    counts = jax.random.randint(first_key, (N_DOM * N_DOM,), 0, BMAX + 1)
    chosen = jax.random.randint(second_key, (), 0, N_DOM * N_DOM)
    counts = jnp.where(jnp.arange(N_DOM * N_DOM) == chosen, BMAX, counts)
    return counts.reshape(N_DOM, N_DOM).astype(jnp.int32)


def draw_edge_count(key, part):
    base_key = jax.random.fold_in(key, 7201)
    first_key, second_key = jax.random.split(base_key)
    capacity = ETILES * EDGE_TILE
    counts = jax.random.randint(first_key, (N_DOM,), capacity // 4, capacity + 1)
    chosen = jax.random.randint(second_key, (), 0, N_DOM)
    counts = jnp.where(jnp.arange(N_DOM) == chosen, capacity, counts)
    return counts.astype(jnp.int32)


def plant(drawn, own_key, low, top_value):
    longest = drawn.shape.index(max(drawn.shape))
    spots = []
    for shift in (0, 1):
        where = [jax.random.randint(jax.random.fold_in(own_key, axis), (), 0, length) for axis, length in enumerate(drawn.shape)]
        where[longest] = (where[longest] + shift) % drawn.shape[longest]
        spots.append(tuple(where))
    return drawn.at[spots[0]].set(low).at[spots[1]].set(top_value)


def block_scale(stream_key, shape, cuts, low, high):
    level = 1.0
    for axis_at, parts in cuts:
        steps = jax.random.uniform(jax.random.fold_in(jax.random.fold_in(stream_key, 6), axis_at), (parts,), jnp.float32, low / len(cuts), high / len(cuts))
        level = level * jnp.repeat(jnp.exp(steps), shape[axis_at] // parts).reshape((-1,) + (1,) * (len(shape) - 1 - axis_at))
    return level


def bell_draw(key, shape, scale, most, pieces=(), held_as=jnp.bfloat16):
    array = scale * jax.random.normal(key, shape, jnp.float32)
    if pieces:
        array = array * block_scale(key, shape, pieces, -0.22, 0.18)
    return jnp.clip(array, -most, most).astype(held_as)


def setup_inputs(seed: int = 0, part: int = 0) -> dict:
    streams_of = jax.random.split(jax.random.key(seed), 20)
    part_splits = jax.random.split(jax.random.fold_in(streams_of[19], part), 20)
    return {
        "node_feats": bell_draw(part_splits[0], (NODES, D), 1.0, 6.0, ((0, 16),), jnp.float32),
        "norm_gain": jnp.clip(1.0 + 0.18 * jax.random.normal(streams_of[1], (D,), jnp.float32), 0.1, 1.9),
        "w_query": draw_w_query(jax.random.fold_in(streams_of[19], 71), part),
        "w_key": draw_w_key(jax.random.fold_in(streams_of[19], 71), part),
        "w_value": bell_draw(streams_of[4], (D, D), D ** -0.5, 0.375),
        "w_out": bell_draw(streams_of[5], (D, D), (D // 4) ** -0.5, 0.75),
        "msg_src_w": bell_draw(streams_of[6], (D, D), (2 * D) ** -0.5, 0.25),
        "msg_dst_w": bell_draw(streams_of[7], (D, D), (2 * D) ** -0.5, 0.25),
        "msg_bias": bell_draw(streams_of[8], (D,), 1.0, 4.0, (), jnp.float32),
        "msg_out_w": bell_draw(streams_of[9], (D, D), (2 * D) ** -0.5, 0.25),
        "msg_out_bias": bell_draw(streams_of[10], (D,), 0.5, 3.0, (), jnp.float32),
        "mlp_gain": jnp.clip(1.0 + 0.18 * jax.random.normal(streams_of[11], (D,), jnp.float32), 0.1, 1.9),
        "mlp_up": bell_draw(streams_of[12], (D, FF), D ** -0.5, 0.375),
        "mlp_down": bell_draw(streams_of[13], (FF, D), FF ** -0.5, 0.1875),
        "send_list": plant(jax.random.randint(part_splits[14], (N_DOM, N_DOM, BMAX), 0, NODE_DEV), jax.random.fold_in(part_splits[14], 1), 0, NODE_DEV - 1).astype(jnp.int32),
        "send_count": draw_send_count(jax.random.fold_in(jax.random.fold_in(streams_of[19], part), 71), part),
        "edge_src": plant(jax.random.randint(part_splits[16], (N_DOM, ETILES, EDGE_TILE), 0, NODE_DEV + N_DOM * BMAX), jax.random.fold_in(part_splits[16], 1), 0, (NODE_DEV + N_DOM * BMAX) - 1).astype(jnp.int32),
        "edge_dst": plant(jax.random.randint(part_splits[17], (N_DOM, ETILES, EDGE_TILE), 0, NODE_DEV), jax.random.fold_in(part_splits[17], 1), 0, NODE_DEV - 1).astype(jnp.int32),
        "edge_count": draw_edge_count(jax.random.fold_in(jax.random.fold_in(streams_of[19], part), 71), part),
    }


def rms_norm(features, scale_gain):
    return features * lax.rsqrt(lax.optimization_barrier(jnp.mean(features * features, axis=-1, keepdims=True)) + 1e-06) * scale_gain.astype(jnp.float32)

def reference(node_feats, norm_gain, w_query, w_key, w_value, w_out, msg_src_w, msg_dst_w, msg_bias, msg_out_w, msg_out_bias, mlp_gain, mlp_up, mlp_down, send_list, send_count, edge_src, edge_dst, edge_count):
    head_size = D // HEADS
    normed = rms_norm(node_feats, norm_gain).astype(jnp.bfloat16)
    queries = jnp.dot(normed, w_query, preferred_element_type=jnp.float32).astype(jnp.bfloat16)
    keys = jnp.dot(normed, w_key, preferred_element_type=jnp.float32).astype(jnp.bfloat16)
    values = jnp.dot(normed, w_value, preferred_element_type=jnp.float32).astype(jnp.bfloat16)
    key_heads = keys.reshape(NODES, HEADS, head_size).astype(jnp.float32)
    value_heads = values.reshape(NODES, HEADS, head_size).astype(jnp.float32)
    query_blocks = queries.reshape(N_DOM, NODE_DEV, HEADS, head_size)

    def attend(query_block):
        scores = jnp.einsum('qhd,khd->hqk', query_block.astype(jnp.float32), key_heads) * head_size ** (-0.5)
        row_max = lax.optimization_barrier(jnp.max(scores, axis=-1, keepdims=True))
        weights = jnp.exp(scores - row_max)
        totals = lax.optimization_barrier(jnp.sum(weights, axis=-1))
        probs = lax.optimization_barrier(weights.astype(jnp.bfloat16)).astype(jnp.float32)
        mixed = jnp.einsum('hqk,khd->qhd', probs, value_heads)
        return (mixed / jnp.transpose(totals)[:, :, None]).astype(jnp.bfloat16)
    attended = lax.map(attend, query_blocks).reshape(NODES, D)
    global_part = jnp.dot(attended, w_out, preferred_element_type=jnp.float32)
    device_ids = jnp.arange(N_DOM, dtype=jnp.int32)[:, None, None]
    is_local = edge_src < NODE_DEV
    slot_index = jnp.maximum(edge_src - NODE_DEV, 0).astype(jnp.int32)
    sender = (slot_index // BMAX).astype(jnp.int32)
    lane_slot = (slot_index % BMAX).astype(jnp.int32)
    device_full = jnp.broadcast_to(device_ids, edge_src.shape)
    remote_row = send_list[sender, device_full, lane_slot]
    source = jnp.where(is_local, device_full * NODE_DEV + edge_src, sender * NODE_DEV + remote_row).astype(jnp.int32)
    slot_live = is_local | (lane_slot < send_count[sender, device_full])
    positions = jnp.arange(ETILES, dtype=jnp.int32)[:, None] * EDGE_TILE + jnp.arange(EDGE_TILE, dtype=jnp.int32)[None, :]
    edge_live = slot_live & (positions[None, :, :] < edge_count[:, None, None])
    destination = (device_full * NODE_DEV + edge_dst).astype(jnp.int32).reshape(-1)
    src_feats = normed[source.reshape(-1)]
    dst_feats = normed[destination]
    pre_act = jnp.dot(src_feats, msg_src_w, preferred_element_type=jnp.float32) + jnp.dot(dst_feats, msg_dst_w, preferred_element_type=jnp.float32) + msg_bias.astype(jnp.float32)
    hidden = jax.nn.silu(pre_act).astype(jnp.bfloat16)
    message = (jnp.dot(hidden, msg_out_w, preferred_element_type=jnp.float32) + msg_out_bias.astype(jnp.float32)).astype(jnp.bfloat16)
    message = jnp.where(edge_live.reshape(-1)[:, None], message.astype(jnp.float32), jnp.zeros((), jnp.float32))
    local_part = jax.ops.segment_sum(message, destination, num_segments=NODES)
    mid = node_feats + local_part + global_part
    mid_normed = rms_norm(mid, mlp_gain).astype(jnp.bfloat16)
    lifted = jax.nn.gelu(jnp.dot(mid_normed, mlp_up, preferred_element_type=jnp.float32)).astype(jnp.bfloat16)
    return mid + jnp.dot(lifted, mlp_down, preferred_element_type=jnp.float32)
```

```python
import functools
import math

import jax
import jax.numpy as jnp
from jax import lax
from jax.experimental import pallas as pl
from jax.experimental.pallas import tpu as pltpu
from jax.sharding import PartitionSpec as P

HEADS = 8
MESH = pl.DeviceIdType.MESH
BF16 = jnp.bfloat16
F32 = jnp.float32


def dot(a, b, dims=((1,), (0,))):
    return lax.dot_general(a, b, (dims, ((), ())), preferred_element_type=F32)


def rms_norm(features, gain):
    return features * lax.rsqrt(jnp.mean(features * features, axis=-1, keepdims=True) + 1e-06) * gain


def kernel(
    n_dom,
    gain_ref,
    msg_bias_ref,
    msg_out_bias_ref,
    mlp_gain_ref,
    list_ref,
    count_ref,
    src_ref,
    dst_ref,
    limit_ref,
    feats_hbm,
    wq_hbm,
    wk_hbm,
    msrc_hbm,
    mdst_hbm,
    mout_hbm,
    wv_hbm,
    wo_hbm,
    up_hbm,
    down_hbm,
    out_ref,
    feats,
    wq,
    wk,
    msrc,
    mdst,
    mout,
    wv,
    wo,
    up,
    down,
    gathered,
    list_out,
    list_in,
    wanted_ref,
    qk,
    acc,
    top,
    total,
    table,
    onehot_src,
    onehot_dst,
    load_sem,
    ring_send,
    ring_recv,
    half_send,
    half_recv,
    pair_send,
    pair_recv,
    list_send,
    list_recv,
):
    rows, width = feats.shape
    depth = list_ref.shape[-1]
    slots = n_dom * depth
    lanes = table.shape[0]
    chips = n_dom // 2
    half = chips // 2
    mid_row = rows // 2
    head = width // HEADS

    sources = (feats_hbm, wq_hbm, wk_hbm, msrc_hbm, mdst_hbm, mout_hbm, wv_hbm, wo_hbm, up_hbm, down_hbm)
    targets = (feats, wq, wk, msrc, mdst, mout, wv, wo, up, down)
    loads = [
        pltpu.make_async_copy(s, t, load_sem.at[i]) for i, (s, t) in enumerate(zip(sources, targets))
    ]
    for load in loads:
        load.start()

    me = lax.axis_index("dom")
    core = lax.rem(me, 2)
    chip = me // 2
    odd = lax.rem(chip, 2)
    pos = (1 - odd) * (chip // 2) + odd * (chips - 1 - chip // 2)

    def device_at(p):
        back = p // half
        return ((1 - back) * (2 * p) + back * (2 * (chips - 1 - p) + 1)) * 2 + core

    right = device_at(lax.rem(pos + 1, chips))
    left = device_at(lax.rem(pos + chips - 1, chips))
    pair = chip * 2 + 1 - core

    barrier = pltpu.get_barrier_semaphore()
    for k in range(1, n_dom):
        pl.semaphore_signal(barrier, inc=1, device_id={"dom": lax.rem(me + k, n_dom)}, device_id_type=MESH)

    lane = lax.broadcasted_iota(jnp.int32, (n_dom, lanes), 1)
    entries = jnp.zeros((n_dom, lanes), jnp.int32)
    lists = list_ref[0]
    for j in range(depth):
        entries = jnp.where(lane == me * depth + j, lists[:, j : j + 1], entries)
    for r in range(n_dom):
        list_out[r] = entries[r : r + 1, :]

    loads[0].wait()
    normed = rms_norm(feats[...], gain_ref[...]).astype(BF16)
    gathered[0, 0] = normed

    pl.semaphore_wait(barrier, n_dom - 1)

    def ring_copy(source, target, device):
        return pltpu.make_async_remote_copy(
            src_ref=gathered.at[source, 0],
            dst_ref=gathered.at[target, 0],
            send_sem=ring_send.at[target],
            recv_sem=ring_recv.at[target],
            device_id={"dom": device},
            device_id_type=MESH,
        )

    def half_copy(source, which, device):
        part = pl.ds(which * mid_row, mid_row)
        return pltpu.make_async_remote_copy(
            src_ref=gathered.at[source, 0, part],
            dst_ref=gathered.at[half, 0, part],
            send_sem=half_send.at[which],
            recv_sem=half_recv.at[which],
            device_id={"dom": device},
            device_id_type=MESH,
        )

    def pair_copy(slot):
        return pltpu.make_async_remote_copy(
            src_ref=gathered.at[slot, 0],
            dst_ref=gathered.at[slot, 1],
            send_sem=pair_send.at[slot],
            recv_sem=pair_recv.at[slot],
            device_id={"dom": pair},
            device_id_type=MESH,
        )

    def list_copy(k):
        to = lax.rem(me + k, n_dom)
        return pltpu.make_async_remote_copy(
            src_ref=list_out.at[to],
            dst_ref=list_in.at[k],
            send_sem=list_send.at[k],
            recv_sem=list_recv.at[k],
            device_id={"dom": to},
            device_id_type=MESH,
        )

    ring_copy(0, 1, right).start()
    ring_copy(0, chips - 1, left).start()
    pair_copy(0).start()
    for k in range(1, n_dom):
        list_copy(k).start()

    loads[1].wait()
    loads[2].wait()
    queries = dot(normed, wq[...]).astype(BF16)
    column = lax.broadcasted_iota(jnp.int32, (rows, width), 1)
    spread = jnp.concatenate(
        [jnp.where(column // head == h, queries, jnp.zeros_like(queries)) for h in range(HEADS)], axis=0
    )
    factor = head ** (-0.5) * math.log2(math.e)
    qk[...] = (dot(wk[...], spread, ((1,), (1,))) * factor).astype(BF16)

    span = qk.shape[1]
    step_columns = min(span, 2 * rows)

    def attend(block, first):
        for begin in range(0, span, step_columns):
            cols = pl.ds(begin, step_columns)
            scores = dot(block, qk[:, cols])
            block_top = jnp.max(scores, axis=0, keepdims=True)
            if first:
                new_top = block_top
            else:
                new_top = jnp.maximum(top[:, cols], block_top)
            weights = jnp.exp2(scores - new_top)
            sums = jnp.sum(weights, axis=0, keepdims=True)
            mixed = dot(block, weights.astype(BF16), ((0,), (0,)))
            if first:
                total[:, cols] = sums
                acc[:, cols] = mixed
            else:
                rescale = jnp.exp2(top[:, cols] - new_top)
                total[:, cols] = total[:, cols] * rescale + sums
                acc[:, cols] = acc[:, cols] * rescale + mixed
            top[:, cols] = new_top

    row_id = lax.broadcasted_iota(jnp.int32, (rows, lanes), 0)

    def pick(block, places):
        chosen = jnp.concatenate(
            [
                jnp.where(row_id + (offset * 2 + side) * rows == wanted_ref[...], 1.0, 0.0).astype(BF16)
                for offset, side in places
            ],
            axis=0,
        )
        return dot(chosen, block, ((0,), (0,)))

    def blocks_at(places):
        return jnp.concatenate([gathered[offset, side] for offset, side in places], axis=0)

    attend(normed, True)

    tiles, tile = src_ref.shape[1], src_ref.shape[2]
    source_rows = rows + lanes
    limit = limit_ref[0]
    slot_lane = lax.broadcasted_iota(jnp.int32, (n_dom, lanes), 1)
    slot_owner = lax.broadcasted_iota(jnp.int32, (n_dom, lanes), 0)
    counts = jnp.sum(
        jnp.where(slot_lane // depth == slot_owner, count_ref[...], 0), axis=0, keepdims=True
    )
    lane_row = lax.broadcasted_iota(jnp.int32, (1, lanes), 1)
    slot_live = jnp.where(
        (lax.rem(lane_row, depth) < counts) & (lane_row < slots), 1.0, 0.0
    ).astype(BF16)
    valid = jnp.broadcast_to(
        jnp.concatenate([jnp.ones((1, rows), BF16), slot_live], axis=1).astype(F32), (16, source_rows)
    ).astype(BF16)
    source_id = lax.broadcasted_iota(jnp.int32, (source_rows, tile), 0)
    node_id = lax.broadcasted_iota(jnp.int32, (rows, tile), 0)
    edge_lane = lax.broadcasted_iota(jnp.int32, (1, tile), 1)
    for t in range(tiles):
        cols = pl.ds(t * tile, tile)
        src = src_ref[0, t : t + 1, :]
        dst = dst_ref[0, t : t + 1, :]
        hot = jnp.where(source_id == src, 1.0, 0.0).astype(BF16)
        onehot_src[0:source_rows, cols] = hot
        onehot_src[source_rows : source_rows + rows, cols] = jnp.where(node_id == dst, 1.0, 0.0).astype(BF16)
        live = dot(valid, hot)[0:1, :]
        kept = jnp.where(edge_lane + t * tile < limit, live, 0.0)
        onehot_dst[:, cols] = jnp.where(node_id == dst, kept, 0.0).astype(BF16)

    for k in range(1, n_dom):
        list_copy(k).wait()
    asked = jnp.sum(jnp.where(slot_owner == me, entries, 0), axis=0, keepdims=True)
    for k in range(1, n_dom):
        asked = asked + list_in[k]
    owner = lane_row // depth
    owner_chip = owner // 2
    owner_odd = lax.rem(owner_chip, 2)
    owner_pos = (1 - owner_odd) * (owner_chip // 2) + owner_odd * (chips - 1 - owner_chip // 2)
    offset = pos - owner_pos
    offset = jnp.where(offset < 0, offset + chips, offset)
    side = jnp.where(lax.rem(owner, 2) == core, 0, 1)
    wanted_ref[...] = jnp.where(lane_row < slots, (offset * 2 + side) * rows + asked, -1)
    table[...] = pick(normed, [(0, 0)])

    def arrive(h):
        ring_copy(0, h, right).wait_recv()
        ring_copy(0, chips - h, left).wait_recv()

    def work(places):
        block = blocks_at(places)
        attend(block, False)
        table[...] += pick(block, places)

    def hop(h, last):
        ring_copy(0, h, right).wait_recv()
        if last:
            half_copy(h, 0, right).start()
        else:
            ring_copy(h, h + 1, right).start()
        pair_copy(h).start()
        ring_copy(0, chips - h, left).wait_recv()
        if last:
            half_copy(chips - h, 1, left).start()
        else:
            ring_copy(chips - h, chips - h - 1, left).start()
        pair_copy(chips - h).start()

    hop(1, half == 2)
    pair_copy(0).wait_recv()
    work([(1, 0), (chips - 1, 0), (0, 1)])

    def middle(h, last):
        hop(h, last)
        pair_copy(h - 1).wait_recv()
        pair_copy(chips - h + 1).wait_recv()
        work([(h, 0), (chips - h, 0), (h - 1, 1), (chips - h + 1, 1)])

    if half > 3:

        @pl.loop(2, half - 1)
        def _(h):
            middle(h, False)

    if half > 2:
        middle(half - 1, True)

    half_copy(0, 0, right).wait_recv()
    half_copy(0, 1, left).wait_recv()
    pair_copy(half).start()
    pair_copy(half - 1).wait_recv()
    pair_copy(half + 1).wait_recv()
    work([(half, 0), (half - 1, 1), (half + 1, 1)])
    for load in loads[3:]:
        load.wait()
    pair_copy(half).wait_recv()
    work([(half, 1)])

    own_source = dot(normed, msrc[...]).astype(BF16)
    far_source = dot(table[...].astype(BF16), msrc[...]).astype(BF16)
    own_dest = (dot(normed, mdst[...]) + msg_bias_ref[...]).astype(BF16)
    ends = jnp.concatenate([own_source, far_source, own_dest], axis=0)
    hidden = jax.nn.silu(dot(ends, onehot_src[...], ((0,), (0,)))).astype(BF16)
    chosen = onehot_dst[...]
    summed = dot(chosen, hidden, ((1,), (1,)))
    live_edges = jnp.sum(chosen.astype(F32), axis=1, keepdims=True)
    high = summed.astype(BF16)
    low = (summed - high.astype(F32)).astype(BF16)
    local_part = dot(high, mout[...]) + dot(low, mout[...]) + live_edges * msg_out_bias_ref[...]

    mixed = dot(wv[...], acc[...].astype(BF16), ((0,), (0,)))
    attended = jnp.concatenate(
        [
            mixed[h * head : (h + 1) * head, h * rows : (h + 1) * rows] / total[:, h * rows : (h + 1) * rows]
            for h in range(HEADS)
        ],
        axis=0,
    ).astype(BF16)
    mid = feats[...] + local_part + dot(attended, wo[...], ((0,), (0,)))
    mid_normed = rms_norm(mid, mlp_gain_ref[...]).astype(BF16)
    lifted = jax.nn.gelu(dot(mid_normed, up[...])).astype(BF16)
    out_ref[...] = mid + dot(lifted, down[...])

    for target in range(1, chips):
        if target != half:
            ring_copy(0, target, right).wait_send()
    for which in range(2):
        half_copy(0, which, right).wait_send()
    for slot in range(chips):
        pair_copy(slot).wait_send()


def body(
    node_feats,
    norm_gain,
    w_query,
    w_key,
    w_value,
    w_out,
    msg_src_w,
    msg_dst_w,
    msg_bias,
    msg_out_w,
    msg_out_bias,
    mlp_gain,
    mlp_up,
    mlp_down,
    send_list,
    send_count,
    edge_src,
    edge_dst,
    edge_count,
):
    rows, width = node_feats.shape
    n_dom = send_list.shape[1]
    chips = n_dom // 2
    slots = n_dom * send_list.shape[2]
    lanes = -(-slots // 128) * 128
    edges = edge_src.shape[1] * edge_src.shape[2]
    span = HEADS * rows
    large = (node_feats, w_query, w_key, msg_src_w, msg_dst_w, msg_out_w, w_value, w_out, mlp_up, mlp_down)
    vmem = pl.BlockSpec(memory_space=pltpu.VMEM)
    smem = pl.BlockSpec(memory_space=pltpu.SMEM)
    anywhere = pl.BlockSpec(memory_space=pl.ANY)
    dma = pltpu.SemaphoreType.DMA
    return pl.pallas_call(
        functools.partial(kernel, n_dom),
        out_shape=jax.ShapeDtypeStruct((rows, width), F32),
        in_specs=[vmem] * 8 + [smem] + [anywhere] * len(large),
        out_specs=vmem,
        scratch_shapes=[pltpu.VMEM(a.shape, a.dtype) for a in large]
        + [
            pltpu.VMEM((chips, 2, rows, width), BF16),
            pltpu.VMEM((n_dom, 1, lanes), jnp.int32),
            pltpu.VMEM((n_dom, 1, lanes), jnp.int32),
            pltpu.VMEM((1, lanes), jnp.int32),
            pltpu.VMEM((width, span), BF16),
            pltpu.VMEM((width, span), F32),
            pltpu.VMEM((1, span), F32),
            pltpu.VMEM((1, span), F32),
            pltpu.VMEM((lanes, width), F32),
            pltpu.VMEM((2 * rows + lanes, edges), BF16),
            pltpu.VMEM((rows, edges), BF16),
            dma((len(large),)),
            dma((chips,)),
            dma((chips,)),
            dma((2,)),
            dma((2,)),
            dma((chips,)),
            dma((chips,)),
            dma((n_dom,)),
            dma((n_dom,)),
        ],
        compiler_params=pltpu.CompilerParams(
            collective_id=0, has_side_effects=True, vmem_limit_bytes=40 * 1024 * 1024
        ),
    )(
        norm_gain.reshape(1, width),
        msg_bias.reshape(1, width),
        msg_out_bias.reshape(1, width),
        mlp_gain.reshape(1, width),
        send_list,
        send_count,
        edge_src,
        edge_dst,
        edge_count,
        *large,
    )


def solution(mesh):
    nodes = P(("graphs", "dom"), None)
    tiled = P(("graphs", "dom"), None, None)
    return jax.shard_map(
        body,
        mesh=mesh,
        in_specs=(nodes,) + (P(),) * 13 + (tiled, P("graphs", "dom"), tiled, tiled, P(("graphs", "dom"))),
        out_specs=nodes,
        check_vma=False,
    )
```

```python
import functools
import math

import jax
import jax.numpy as jnp
from jax import lax
from jax.experimental import pallas as pl
from jax.experimental.pallas import tpu as pltpu
from jax.sharding import PartitionSpec as P

HEADS = 8
MESH = pl.DeviceIdType.MESH
BF16 = jnp.bfloat16
F32 = jnp.float32


def dot(a, b, dims=((1,), (0,))):
    return lax.dot_general(a, b, (dims, ((), ())), preferred_element_type=F32)


def exact_dot(a, b, dims=((1,), (0,))):
    return lax.dot_general(
        a, b, (dims, ((), ())), preferred_element_type=F32, precision=lax.Precision.HIGHEST
    )


def rms_norm(features, gain):
    return features * lax.rsqrt(jnp.mean(features * features, axis=-1, keepdims=True) + 1e-06) * gain


def kernel(
    n_dom,
    count,
    *refs,
):
    sources, out_ref, targets = refs[:count], refs[count], refs[count + 1 : 2 * count + 1]
    run(n_dom, sources, out_ref, targets, *refs[2 * count + 1 :])


def run(
    n_dom,
    sources,
    out_ref,
    targets,
    gathered,
    list_out,
    list_in,
    wanted_ref,
    qk,
    acc,
    top,
    total,
    table,
    onehot_src,
    onehot_dst,
    load_sem,
    ring_send,
    ring_recv,
    half_send,
    half_recv,
    pair_send,
    pair_recv,
    list_send,
    list_recv,
):
    (
        feats,
        gain_ref,
        list_ref,
        wq,
        wk,
        count_ref,
        src_ref,
        dst_ref,
        limit_ref,
        msrc,
        mdst,
        msg_bias_ref,
        mout,
        msg_out_bias_ref,
        wv,
        wo,
        mlp_gain_ref,
        up,
        down,
    ) = targets
    rows, width = feats.shape
    depth = list_ref.shape[1]
    slots = n_dom * depth
    lanes = table.shape[0]
    chips = n_dom // 2
    half = chips // 2
    mid_row = rows // 2
    head = width // HEADS

    loads = [
        pltpu.make_async_copy(s, t, load_sem.at[i]) for i, (s, t) in enumerate(zip(sources, targets))
    ]
    for load in loads:
        load.start()

    me = lax.axis_index("dom")
    core = lax.rem(me, 2)
    chip = me // 2
    odd = lax.rem(chip, 2)
    pos = (1 - odd) * (chip // 2) + odd * (chips - 1 - chip // 2)

    def device_at(p):
        back = p // half
        return ((1 - back) * (2 * p) + back * (2 * (chips - 1 - p) + 1)) * 2 + core

    right = device_at(lax.rem(pos + 1, chips))
    left = device_at(lax.rem(pos + chips - 1, chips))
    pair = chip * 2 + 1 - core

    barrier = pltpu.get_barrier_semaphore()
    for k in range(1, n_dom):
        pl.semaphore_signal(barrier, inc=1, device_id={"dom": lax.rem(me + k, n_dom)}, device_id_type=MESH)

    loads[0].wait()
    loads[1].wait()
    normed = rms_norm(feats[...], gain_ref[...]).astype(BF16)
    gathered[0, 0] = normed
    loads[2].wait()
    place = lax.broadcasted_iota(jnp.int32, (depth, lanes), 1) - me * depth
    place = place == lax.broadcasted_iota(jnp.int32, (depth, lanes), 0)
    entries = exact_dot(
        list_ref[0].astype(F32), jnp.where(place, 1.0, 0.0), ((0,), (0,))
    ).astype(jnp.int32)
    for r in range(n_dom):
        list_out[r] = entries[r : r + 1, :]

    pl.semaphore_wait(barrier, n_dom - 1)

    def ring_copy(source, target, device):
        return pltpu.make_async_remote_copy(
            src_ref=gathered.at[source, 0],
            dst_ref=gathered.at[target, 0],
            send_sem=ring_send.at[target],
            recv_sem=ring_recv.at[target],
            device_id={"dom": device},
            device_id_type=MESH,
        )

    def half_copy(source, which, device):
        part = pl.ds(which * mid_row, mid_row)
        return pltpu.make_async_remote_copy(
            src_ref=gathered.at[source, 0, part],
            dst_ref=gathered.at[half, 0, part],
            send_sem=half_send.at[which],
            recv_sem=half_recv.at[which],
            device_id={"dom": device},
            device_id_type=MESH,
        )

    def pair_copy(slot):
        return pltpu.make_async_remote_copy(
            src_ref=gathered.at[slot, 0],
            dst_ref=gathered.at[slot, 1],
            send_sem=pair_send.at[slot],
            recv_sem=pair_recv.at[slot],
            device_id={"dom": pair},
            device_id_type=MESH,
        )

    def list_copy(k):
        to = lax.rem(me + k, n_dom)
        return pltpu.make_async_remote_copy(
            src_ref=list_out.at[to],
            dst_ref=list_in.at[k],
            send_sem=list_send.at[k],
            recv_sem=list_recv.at[k],
            device_id={"dom": to},
            device_id_type=MESH,
        )

    ring_copy(0, 1, right).start()
    ring_copy(0, chips - 1, left).start()
    pair_copy(0).start()
    for k in range(1, n_dom):
        list_copy(k).start()

    loads[3].wait()
    loads[4].wait()
    queries = dot(normed, wq[...]).astype(BF16)
    column = lax.broadcasted_iota(jnp.int32, (rows, width), 1)
    spread = jnp.concatenate(
        [jnp.where(column // head == h, queries, jnp.zeros_like(queries)) for h in range(HEADS)], axis=0
    )
    factor = head ** (-0.5) * math.log2(math.e)
    qk[...] = (dot(wk[...], spread, ((1,), (1,))) * factor).astype(BF16)

    span = qk.shape[1]
    step_columns = min(span, 2 * rows)

    def attend(block, first):
        turned = jnp.transpose(block)
        for begin in range(0, span, step_columns):
            cols = pl.ds(begin, step_columns)
            scores = dot(block, qk[:, cols])
            block_top = jnp.max(scores, axis=0, keepdims=True)
            if first:
                new_top = block_top
            else:
                new_top = jnp.maximum(top[:, cols], block_top)
            weights = jnp.exp2(scores - new_top)
            sums = jnp.sum(weights, axis=0, keepdims=True)
            mixed = dot(turned, weights.astype(BF16))
            if first:
                total[:, cols] = sums
                acc[:, cols] = mixed
            else:
                rescale = jnp.exp2(top[:, cols] - new_top)
                total[:, cols] = total[:, cols] * rescale + sums
                acc[:, cols] = acc[:, cols] * rescale + mixed
            top[:, cols] = new_top

    row_id = lax.broadcasted_iota(jnp.int32, (rows, lanes), 0)

    def pick(block, places):
        chosen = jnp.concatenate(
            [
                jnp.where(row_id + (offset * 2 + side) * rows == wanted_ref[...], 1.0, 0.0).astype(BF16)
                for offset, side in places
            ],
            axis=0,
        )
        return dot(chosen, block, ((0,), (0,)))

    def blocks_at(places):
        return jnp.concatenate([gathered[offset, side] for offset, side in places], axis=0)

    attend(normed, True)
    for load in loads[5:9]:
        load.wait()

    tiles, tile = src_ref.shape[1], src_ref.shape[2]
    source_rows = rows + lanes
    limit = limit_ref[...]
    slot_lane = lax.broadcasted_iota(jnp.int32, (n_dom, lanes), 1)
    slot_owner = lax.broadcasted_iota(jnp.int32, (n_dom, lanes), 0)
    counts = exact_dot(
        jnp.broadcast_to(count_ref[...], (8, n_dom)).astype(F32),
        jnp.where(slot_lane // depth == slot_owner, 1.0, 0.0),
    )[0:1, :].astype(jnp.int32)
    lane_row = lax.broadcasted_iota(jnp.int32, (1, lanes), 1)
    slot_live = jnp.where(
        (lax.rem(lane_row, depth) < counts) & (lane_row < slots), 1.0, 0.0
    ).astype(BF16)
    valid = jnp.broadcast_to(
        jnp.concatenate([jnp.ones((1, rows), BF16), slot_live], axis=1).astype(F32), (16, source_rows)
    ).astype(BF16)
    source_id = lax.broadcasted_iota(jnp.int32, (source_rows, tile), 0)
    node_id = lax.broadcasted_iota(jnp.int32, (rows, tile), 0)
    edge_lane = lax.broadcasted_iota(jnp.int32, (1, tile), 1)
    for t in range(tiles):
        cols = pl.ds(t * tile, tile)
        src = src_ref[0, t : t + 1, :]
        dst = dst_ref[0, t : t + 1, :]
        hot = jnp.where(source_id == src, 1.0, 0.0).astype(BF16)
        onehot_src[0:source_rows, cols] = hot
        onehot_src[source_rows : source_rows + rows, cols] = jnp.where(node_id == dst, 1.0, 0.0).astype(BF16)
        live = dot(valid, hot)[0:1, :]
        kept = jnp.where(edge_lane + t * tile < limit, live, 0.0)
        onehot_dst[:, cols] = jnp.where(node_id == dst, kept, 0.0).astype(BF16)

    for k in range(1, n_dom):
        list_copy(k).wait()
    asked = jnp.sum(jnp.where(slot_owner == me, entries, 0), axis=0, keepdims=True)
    for k in range(1, n_dom):
        asked = asked + list_in[k]
    owner = lane_row // depth
    owner_chip = owner // 2
    owner_odd = lax.rem(owner_chip, 2)
    owner_pos = (1 - owner_odd) * (owner_chip // 2) + owner_odd * (chips - 1 - owner_chip // 2)
    offset = pos - owner_pos
    offset = jnp.where(offset < 0, offset + chips, offset)
    side = jnp.where(lax.rem(owner, 2) == core, 0, 1)
    wanted_ref[...] = jnp.where(lane_row < slots, (offset * 2 + side) * rows + asked, -1)
    table[...] = pick(normed, [(0, 0)])

    def work(places):
        block = blocks_at(places)
        attend(block, False)
        table[...] += pick(block, places)

    def hop(h, last):
        ring_copy(0, h, right).wait_recv()
        if last:
            half_copy(h, 0, right).start()
        else:
            ring_copy(h, h + 1, right).start()
        pair_copy(h).start()
        ring_copy(0, chips - h, left).wait_recv()
        if last:
            half_copy(chips - h, 1, left).start()
        else:
            ring_copy(chips - h, chips - h - 1, left).start()
        pair_copy(chips - h).start()

    hop(1, half == 2)
    pair_copy(0).wait_recv()
    work([(1, 0), (chips - 1, 0), (0, 1)])

    def middle(h, last):
        hop(h, last)
        pair_copy(h - 1).wait_recv()
        pair_copy(chips - h + 1).wait_recv()
        work([(h, 0), (chips - h, 0), (h - 1, 1), (chips - h + 1, 1)])

    if half > 3:

        @pl.loop(2, half - 1)
        def _(h):
            middle(h, False)

    if half > 2:
        middle(half - 1, True)

    half_copy(0, 0, right).wait_recv()
    half_copy(0, 1, left).wait_recv()
    pair_copy(half).start()
    pair_copy(half - 1).wait_recv()
    pair_copy(half + 1).wait_recv()
    work([(half, 0), (half - 1, 1), (half + 1, 1)])
    for load in loads[9:]:
        load.wait()
    pair_copy(half).wait_recv()
    work([(half, 1)])

    own_source = dot(normed, msrc[...]).astype(BF16)
    far_source = dot(table[...].astype(BF16), msrc[...]).astype(BF16)
    own_dest = (dot(normed, mdst[...]) + msg_bias_ref[...]).astype(BF16)
    ends = jnp.concatenate([own_source, far_source, own_dest], axis=0)
    hidden = jax.nn.silu(dot(ends, onehot_src[...], ((0,), (0,)))).astype(BF16)
    chosen = onehot_dst[...]
    summed = dot(chosen, hidden, ((1,), (1,)))
    live_edges = jnp.sum(chosen.astype(F32), axis=1, keepdims=True)
    high = summed.astype(BF16)
    low = (summed - high.astype(F32)).astype(BF16)
    local_part = dot(high, mout[...]) + dot(low, mout[...]) + live_edges * msg_out_bias_ref[...]

    mixed = dot(wv[...], acc[...].astype(BF16), ((0,), (0,)))
    attended = jnp.concatenate(
        [
            mixed[h * head : (h + 1) * head, h * rows : (h + 1) * rows] / total[:, h * rows : (h + 1) * rows]
            for h in range(HEADS)
        ],
        axis=0,
    ).astype(BF16)
    mid = feats[...] + local_part + dot(attended, wo[...], ((0,), (0,)))
    mid_normed = rms_norm(mid, mlp_gain_ref[...]).astype(BF16)
    lifted = jax.nn.gelu(dot(mid_normed, up[...])).astype(BF16)
    out_ref[...] = mid + dot(lifted, down[...])

    for target in range(1, chips):
        if target != half:
            ring_copy(0, target, right).wait_send()
    for which in range(2):
        half_copy(0, which, right).wait_send()
    for slot in range(chips):
        pair_copy(slot).wait_send()


def body(
    node_feats,
    norm_gain,
    w_query,
    w_key,
    w_value,
    w_out,
    msg_src_w,
    msg_dst_w,
    msg_bias,
    msg_out_w,
    msg_out_bias,
    mlp_gain,
    mlp_up,
    mlp_down,
    send_list,
    send_count,
    edge_src,
    edge_dst,
    edge_count,
):
    rows, width = node_feats.shape
    n_dom = send_list.shape[1]
    chips = n_dom // 2
    slots = n_dom * send_list.shape[2]
    lanes = -(-slots // 128) * 128
    edges = edge_src.shape[1] * edge_src.shape[2]
    span = HEADS * rows
    line = lambda vector: vector.reshape(1, -1)
    operands = (
        node_feats,
        line(norm_gain),
        jnp.transpose(send_list, (0, 2, 1)),
        w_query,
        w_key,
        jnp.transpose(send_count),
        edge_src,
        edge_dst,
        line(edge_count),
        msg_src_w,
        msg_dst_w,
        line(msg_bias),
        msg_out_w,
        line(msg_out_bias),
        w_value,
        w_out,
        line(mlp_gain),
        mlp_up,
        mlp_down,
    )
    dma = pltpu.SemaphoreType.DMA
    scratch = [
        pltpu.VMEM((chips, 2, rows, width), BF16),
        pltpu.VMEM((n_dom, 1, lanes), jnp.int32),
        pltpu.VMEM((n_dom, 1, lanes), jnp.int32),
        pltpu.VMEM((1, lanes), jnp.int32),
        pltpu.VMEM((width, span), BF16),
        pltpu.VMEM((width, span), F32),
        pltpu.VMEM((1, span), F32),
        pltpu.VMEM((1, span), F32),
        pltpu.VMEM((lanes, width), F32),
        pltpu.VMEM((2 * rows + lanes, edges), BF16),
        pltpu.VMEM((rows, edges), BF16),
        dma((len(operands),)),
        dma((chips,)),
        dma((chips,)),
        dma((2,)),
        dma((2,)),
        dma((chips,)),
        dma((chips,)),
        dma((n_dom,)),
        dma((n_dom,)),
    ]
    return pl.pallas_call(
        functools.partial(kernel, n_dom, len(operands)),
        out_shape=jax.ShapeDtypeStruct((rows, width), F32),
        in_specs=[pl.BlockSpec(memory_space=pltpu.HBM)] * len(operands),
        out_specs=pl.BlockSpec(memory_space=pltpu.VMEM),
        scratch_shapes=[pltpu.VMEM(a.shape, a.dtype) for a in operands] + scratch,
        compiler_params=pltpu.CompilerParams(
            collective_id=0, has_side_effects=True, vmem_limit_bytes=64 * 1024 * 1024 - 65536
        ),
    )(*operands)


def solution(mesh):
    nodes = P(("graphs", "dom"), None)
    tiled = P(("graphs", "dom"), None, None)
    return jax.shard_map(
        body,
        mesh=mesh,
        in_specs=(nodes,) + (P(),) * 13 + (tiled, P("graphs", "dom"), tiled, tiled, P(("graphs", "dom"))),
        out_specs=nodes,
        check_vma=False,
    )
```
